32 devices in a mesh: sta: 8 (over y, x, core), tm: 4 (over z).
Axes of the slice: x: 2, y: 2, z: 4, core: 2. Of those that a mesh axis runs over, the one named last changes fastest.
Arguments:
- waves: bfloat16 [3, 1024, 4, 512], P(None, 'sta', 'tm'), may hold values from -6 to 6
- partner: int32 [7, 8], replicated, may hold values from 0 to 7, as said below
- pair_count: int32 [8], P('sta'), may hold values from 192 to 256, as said below
- left_station: int32 [8, 256], P('sta'), may hold values from 0 to 127, as said below
- right_station: int32 [8, 256], P('sta'), may hold values from 0 to 127
- owner: int32 [8, 256], P('sta'), may hold values from 0 to 7, as said below
Outputs:
- stacks: float32 [4096, 2304], P('sta', 'tm')
The draws below stay inside these ranges and needn't reach their ends.
Inputs may be any that keep to these rules, and one draw needn't show every extreme that they name: partner[k, i] = i XOR r_k, where r_0, ..., r_(6) are the numbers 1 to 7 in an order drawn from the seed. `pair_count`: each list's count is at least three quarters of 256; some list is full. Within one list the pairs (left_station, right_station) are all different. `owner`: among the first pair_count entries of a list, no block is named more than 64 times; one block, drawn from the seed, is named exactly 64 times in every list.
All inputs are finite; a program needn't handle non-finite values.
Results may differ from the reference program's by a relative error of at most 0.0032.
Values may be sent and summed in bfloat16 or wider, within the bound.
No kernel may reach another device: no remote copies, remote signals or barrier semaphores. Data moves between devices by JAX's collectives and lax.ppermute only.
A program may use at most 64 MiB of HBM per device.

```python
import math
import jax
import jax.numpy as jnp
from jax import lax

STA_DEV = 128
PAIR_CAP = 256
L = 512
LAGS = 256
HALF_BAND = 21
FREQS = 256
STATIONS = 1024
SEGMENTS = 4
CAP = 64
SLOTS = 4096
N_STA = 8


def count_helper(key):
    base = jax.random.fold_in(key, 11)
    drawn = jax.random.randint(base, (N_STA,), 3 * PAIR_CAP // 4, PAIR_CAP + 1)
    full_list = jax.random.randint(jax.random.fold_in(base, 1), (), 0, N_STA)
    return jnp.where(jnp.arange(N_STA) == full_list, PAIR_CAP, drawn).astype(jnp.int32)


def pair_helper(key):
    base = jax.random.fold_in(key, 31)
    list_keys = jax.random.split(base, N_STA)

    def one_list(list_key):
        return jax.random.permutation(list_key, STA_DEV * STA_DEV)[:PAIR_CAP].astype(jnp.int32)
    return jax.vmap(one_list)(list_keys)


def draw_partner(key, part):
    offsets = jax.random.permutation(jax.random.fold_in(key, 21), N_STA - 1).astype(jnp.int32) + 1
    blocks = jnp.arange(N_STA, dtype=jnp.int32)
    return jnp.bitwise_xor(blocks[None, :], offsets[:, None]).astype(jnp.int32)


def draw_pair_count(key, part):
    return count_helper(key)


def draw_left_station(key, part):
    return (pair_helper(key) // STA_DEV).astype(jnp.int32)


def draw_right_station(key, part):
    return (pair_helper(key) % STA_DEV).astype(jnp.int32)


def draw_owner(key, part):
    counts = count_helper(key)
    hot_owner = jax.random.randint(jax.random.fold_in(key, 41), (), 0, N_STA)
    list_keys = jax.random.split(jax.random.fold_in(key, 43), N_STA)

    def one_list(list_key, count):
        pool = jnp.arange((N_STA - 1) * CAP, dtype=jnp.int32) // CAP
        pool = pool + (pool >= hot_owner).astype(jnp.int32)
        pool = jax.random.permutation(jax.random.fold_in(list_key, 1), pool)
        sequence = jnp.concatenate([jnp.full((CAP,), hot_owner, jnp.int32), pool[:PAIR_CAP - CAP]])
        entry = jnp.arange(PAIR_CAP, dtype=jnp.int32)
        ranking = jax.random.permutation(jax.random.fold_in(list_key, 2), PAIR_CAP).astype(jnp.int32)
        sort_keys = ranking + (entry >= count).astype(jnp.int32) * PAIR_CAP
        placing = jnp.argsort(sort_keys, stable=True)
        return jnp.zeros((PAIR_CAP,), jnp.int32).at[placing].set(sequence)
    return jax.vmap(one_list)(list_keys, counts).astype(jnp.int32)


def block_levels(rng, dims, cuts, least, top_value):
    gain, own = 1.0, jax.random.fold_in(rng, 6)
    for position, blocks in cuts:
        steps = jnp.exp(jax.random.uniform(jax.random.fold_in(own, position), (blocks,), jnp.float32, least / len(cuts), top_value / len(cuts)))
        gain = gain * jnp.repeat(steps, dims[position] // blocks).reshape([-1 if axis == position else 1 for axis in range(len(dims))])
    return gain


def noise(stream_key, shape, spread, bound, cuts=(), kind=jnp.bfloat16):
    level = block_levels(stream_key, shape, cuts, -0.22, 0.18) if cuts else 1.0
    array = jax.random.normal(stream_key, shape, jnp.float32) * spread * level
    return jnp.minimum(jnp.maximum(array, -bound), bound).astype(kind)


def setup_inputs(seed: int = 0) -> dict:
    seeds = jax.random.split(jax.random.key(seed), 7)
    waves = noise(seeds[0], (3, STATIONS, SEGMENTS, L), 1.0, 6.0, ((1, 8), (2, 4)))
    partner = draw_partner(jax.random.fold_in(seeds[6], 71), 0)
    pair_count = draw_pair_count(jax.random.fold_in(seeds[6], 71), 0)
    left_station = draw_left_station(jax.random.fold_in(seeds[6], 71), 0)
    right_station = draw_right_station(jax.random.fold_in(seeds[6], 71), 0)
    owner = draw_owner(jax.random.fold_in(seeds[6], 71), 0)
    return dict(waves=waves, partner=partner, pair_count=pair_count, left_station=left_station, right_station=right_station, owner=owner)


epsilon = 1e-06

def make_dft_table(samples, freq_count):
    sample_index = jnp.arange(samples, dtype=jnp.int32)[:, None]
    freq_index = jnp.arange(freq_count, dtype=jnp.int32)[None, :]
    phases = 2.0 * math.pi / samples * jnp.mod(sample_index * freq_index, samples).astype(jnp.float32)
    return jnp.concatenate([jnp.cos(phases), -jnp.sin(phases)], axis=1).astype(jnp.bfloat16)

def make_lag_table(samples, freq_count, lag_count):
    freq_index = jnp.arange(freq_count, dtype=jnp.int32)[:, None]
    lag_index = jnp.arange(lag_count, dtype=jnp.int32)[None, :] - lag_count // 2
    phases = 2.0 * math.pi / samples * jnp.mod(freq_index * lag_index, samples).astype(jnp.float32)
    return jnp.concatenate([jnp.cos(phases), -jnp.sin(phases)], axis=0)

def make_band(freq_count, half_band):
    freq_index = jnp.arange(freq_count, dtype=jnp.int32)
    band_matrix = (jnp.abs(freq_index[:, None] - freq_index[None, :]) <= half_band).astype(jnp.float32)
    return (band_matrix, lax.optimization_barrier(jnp.sum(band_matrix, axis=0)))

def whiten(records, dft_table, band_matrix, band_count):
    dims_in = records.shape
    spectra = jnp.dot(records.reshape(-1, dims_in[-1]), dft_table, preferred_element_type=jnp.float32)
    spectra = spectra.reshape(dims_in[:-1] + (dft_table.shape[1],))
    freq_count = dft_table.shape[1] // 2
    magnitude = jnp.sqrt(spectra[..., :freq_count] ** 2 + spectra[..., freq_count:] ** 2)
    amplitude = lax.optimization_barrier(jnp.sum(magnitude, axis=-4))
    smooth = jnp.dot(amplitude.reshape(-1, freq_count), band_matrix, precision=lax.Precision.HIGHEST)
    smooth = smooth.reshape(amplitude.shape) / (3.0 * band_count) + epsilon
    smooth = jnp.concatenate([smooth, smooth], axis=-1)
    return spectra / jnp.expand_dims(smooth, -4)

def correlate(left_white, right_white, left_index, right_index, lag_table, scale):
    precise = lax.Precision.HIGHEST
    left_rows = jnp.take(left_white, left_index, axis=1)
    right_rows = jnp.take(right_white, right_index, axis=1)
    freq_count = left_rows.shape[-1] // 2
    left_real, left_imag = (left_rows[..., :freq_count], left_rows[..., freq_count:])
    right_real, right_imag = (right_rows[..., :freq_count], right_rows[..., freq_count:])
    cross_real = jnp.einsum('apsf,bpsf->pabf', left_real, right_real, precision=precise) + jnp.einsum('apsf,bpsf->pabf', left_imag, right_imag, precision=precise)
    cross_imag = jnp.einsum('apsf,bpsf->pabf', left_imag, right_real, precision=precise) - jnp.einsum('apsf,bpsf->pabf', left_real, right_imag, precision=precise)
    cross = jnp.concatenate([cross_real, cross_imag], axis=-1)
    lagged = jnp.einsum('pabg,gl->pabl', cross, lag_table, precision=precise) * scale
    return lagged.reshape(lagged.shape[0], -1)

def correlate_list(left_white, right_white, left_index, right_index, lag_table, scale):
    pair_total = left_index.shape[0]
    block_pairs = math.gcd(pair_total, 64)

    def one_block(indices):
        return correlate(left_white, right_white, indices[0], indices[1], lag_table, scale)
    lagged = lax.map(one_block, (left_index.reshape(-1, block_pairs), right_index.reshape(-1, block_pairs)))
    return lagged.reshape(pair_total, -1)

def slot_rows(owner_row, count, blocks, capacity):
    entry = jnp.arange(owner_row.shape[0], dtype=jnp.int32)
    valid = entry < count
    hits = ((owner_row[:, None] == jnp.arange(blocks, dtype=jnp.int32)[None, :]) & valid[:, None]).astype(jnp.int32)
    before = jnp.cumsum(hits, axis=0) - hits
    rank = lax.optimization_barrier(jnp.sum(before * hits, axis=1))
    return (jnp.where(valid, owner_row * capacity + rank, blocks * capacity), valid)

def reference(waves, partner, pair_count, left_station, right_station, owner):
    dft_table = make_dft_table(L, FREQS)
    band_matrix, band_count = make_band(FREQS, HALF_BAND)
    lag_table = make_lag_table(L, FREQS, LAGS)
    scale = 1.0 / math.sqrt(FREQS * SEGMENTS)
    blocked = waves.reshape(3, N_STA, STA_DEV, SEGMENTS, L).transpose(1, 0, 2, 3, 4)
    this_round = partner[0]

    def whiten_block(records):
        return whiten(records, dft_table, band_matrix, band_count)
    white_all = lax.map(whiten_block, blocked)

    def one_list(list_index):
        lagged = correlate_list(white_all[list_index], white_all[this_round[list_index]], left_station[list_index], right_station[list_index], lag_table, scale)
        valid = jnp.arange(PAIR_CAP, dtype=jnp.int32) < pair_count[list_index]
        return jnp.where(valid[:, None], lagged, jnp.zeros_like(lagged))
    stacks_all = lax.map(one_list, jnp.arange(N_STA, dtype=jnp.int32))

    def list_rows(list_index):
        slot, valid = slot_rows(owner[list_index], pair_count[list_index], N_STA, CAP)
        target = slot // CAP * (N_STA * CAP) + list_index * CAP + slot % CAP
        return jnp.where(valid, target, SLOTS).astype(jnp.int32)
    rows = jax.vmap(list_rows)(jnp.arange(N_STA, dtype=jnp.int32))
    stacks = jnp.zeros((SLOTS, 9 * LAGS), jnp.float32)
    return stacks.at[rows.reshape(-1)].add(stacks_all.reshape(-1, 9 * LAGS), mode='drop')
```

```python
import functools
import math

import jax
import jax.numpy as jnp
import numpy as np
from jax import lax
from jax.experimental import pallas as pl
from jax.experimental.pallas import tpu as pltpu
from jax.sharding import PartitionSpec as P

LAGS = 256
HALF_BAND = 21
EPSILON = 1e-06
F32 = jnp.float32
BF16 = jnp.bfloat16
VMEM_LIMIT = 48 * 1024 * 1024


def xor_pairs(count, mask):
    return [(i, i ^ mask) for i in range(count)]


def split(x):
    hi = x.astype(BF16)
    return hi, (x - hi.astype(F32)).astype(BF16)


def tables(samples, freqs, scale):
    n = np.arange(samples, dtype=np.int64)
    f = np.arange(freqs, dtype=np.int64)
    step = np.float32(2.0 * math.pi / samples)
    phase = (step * np.mod(f[:, None] * n[None, :], samples).astype(np.float32)).astype(np.float32)
    dft = np.concatenate([np.cos(phase), -np.sin(phase)], axis=0).astype(jnp.bfloat16)
    lag = np.arange(LAGS, dtype=np.int64) - LAGS // 2
    phase = (step * np.mod(lag[:, None] * f[None, :], samples).astype(np.float32)).astype(np.float32)
    table = np.concatenate([np.cos(phase), -np.sin(phase)], axis=1) * np.float32(scale)
    high = table.astype(jnp.bfloat16)
    low = (table - high.astype(np.float32)).astype(jnp.bfloat16)
    near = np.abs(f[:, None] - f[None, :]) <= HALF_BAND
    inverse = (1.0 / (3.0 * near.sum(axis=1))).astype(np.float32)[:, None]
    return dft, high, low, near.astype(jnp.bfloat16), np.broadcast_to(inverse, (freqs, 128)).copy()


def whiten_rows(x, dft, band, inverse, index):
    stations = x.shape[0] // 3
    freqs = band.shape[0]
    spectra = [
        lax.dot_general(
            dft, x[c * stations : (c + 1) * stations], (((1,), (1,)), ((), ())), preferred_element_type=F32
        )
        for c in range(3)
    ]
    amplitude = sum(jnp.sqrt(s[:freqs] * s[:freqs] + s[freqs:] * s[freqs:]) for s in spectra)
    high, low = split(amplitude)
    smooth = jnp.dot(band, high, preferred_element_type=F32) + jnp.dot(band, low, preferred_element_type=F32)
    factor = 1.0 / (smooth * inverse[:, :1] + EPSILON)
    factor = jnp.concatenate([factor, factor], axis=0)
    pick = lax.broadcasted_iota(jnp.int32, (stations, index.shape[1]), 0) == index
    pick = pick.astype(F32).astype(BF16)
    pick = jnp.concatenate([pick, pick], axis=0)
    rows = []
    for s in spectra:
        high, low = split(s * factor)
        rows.append(jnp.dot(jnp.concatenate([high, low], axis=1), pick, preferred_element_type=F32))
    return rows


def whiten_kernel(x, dft, band, inverse, index, out):
    rows = whiten_rows(x[...], dft[...], band[...], inverse[...], index[...])
    for c in range(3):
        out[c] = rows[c]


def piece_rows(lefts, rights, high_table, low_table, cross_high, cross_low, lagged, piece, width, blocks):
    freqs = lefts[0].shape[1] // 2
    start = piece * width
    first = start // LAGS
    step = 32
    for j in range(blocks):
        ac = jnp.minimum(first + j, 8)
        a, c = ac // 3, ac % 3
        for r in range(0, freqs, step):
            real, imag = 0.0, 0.0
            for left, right in zip(lefts, rights):
                lr, li = left[a, r : r + step], left[a, freqs + r : freqs + r + step]
                rr, ri = right[c, r : r + step], right[c, freqs + r : freqs + r + step]
                real = real + (lr * rr + li * ri)
                imag = imag + (li * rr - lr * ri)
            cross_high[r : r + step], cross_low[r : r + step] = split(real)
            cross_high[freqs + r : freqs + r + step], cross_low[freqs + r : freqs + r + step] = split(imag)
        lagged[j * LAGS : (j + 1) * LAGS] = (
            jnp.dot(high_table[...], cross_high[...], preferred_element_type=F32)
            + jnp.dot(low_table[...], cross_high[...], preferred_element_type=F32)
            + jnp.dot(high_table[...], cross_low[...], preferred_element_type=F32)
        )
    return start - first * LAGS


def send_kernel(
    width, blocks, sends, meta, g0, h0, g1, xa, xb, dft, band, inverse, index, high_table, low_table,
    out, h1, cross_high, cross_low, lagged,
):
    x = jnp.concatenate([xa[...], xb[...]], axis=0)
    rows = whiten_rows(x, dft[...], band[...], inverse[...], index[...])
    for c in range(3):
        h1[c] = rows[c]
    t = meta[0]
    for j in range(sends):
        piece = t ^ (2 * (j + 1))
        shift = piece_rows(
            (g0, g1), (h0, h1), high_table, low_table, cross_high, cross_low, lagged, piece, width, blocks
        )
        out[j] = lagged[pl.ds(pl.multiple_of(shift, 16), width)].astype(BF16)


def own_kernel(
    width, blocks, meta, g0, h0, g1, h1, high_table, low_table, out, cross_high, cross_low, lagged
):
    shift = piece_rows(
        (g0, g1), (h0, h1), high_table, low_table, cross_high, cross_low, lagged, meta[0], width, blocks
    )
    out[...] = lagged[pl.ds(pl.multiple_of(shift, 16), width)]


def total_kernel(own, received, out):
    total = own[...]
    for j in range(received.shape[0]):
        total = total + received[j].astype(F32)
    out[...] = total.astype(BF16)


def slot_lanes(owner, blocks):
    pairs = owner.shape[1]
    hits = lax.broadcasted_iota(jnp.int32, (blocks, pairs), 0) == owner
    hits = hits.astype(F32)
    earlier = lax.broadcasted_iota(jnp.int32, (pairs, pairs), 0) < lax.broadcasted_iota(jnp.int32, (pairs, pairs), 1)
    before = jnp.dot(hits.astype(BF16), earlier.astype(F32).astype(BF16), preferred_element_type=F32)
    return jnp.sum(before * hits, axis=0, keepdims=True).astype(jnp.int32)


def route_kernel(blocks, capacity, meta, total, other, owner, other_owner, *outs):
    chip, core = meta[1], meta[2]
    pairs = owner.shape[1]
    chips = blocks // 2
    picks = []
    for value, lists in ((owner[...], core), (other_owner[...], 1 - core)):
        rank = slot_lanes(value, blocks)
        lane = ((value // 2) ^ chip) * (2 * capacity) + lists * capacity + rank
        mine = jnp.logical_and(value >= 0, value % 2 == core)
        lane = jnp.where(mine, lane, -1)
        slots = lax.broadcasted_iota(jnp.int32, (chips * 2 * capacity, pairs), 0)
        picks.append((slots == lane).astype(F32).astype(BF16))
    values = jnp.concatenate([total[...], other[...]], axis=1)
    pick = jnp.concatenate(picks, axis=1)
    routed = lax.dot_general(values, pick, (((1,), (1,)), ((), ())), preferred_element_type=F32)
    for j in range(chips):
        outs[j][...] = routed[:, j * 2 * capacity : (j + 1) * 2 * capacity].astype(BF16)


def place_kernel(lanes, meta, *refs):
    out = refs[-1]
    chip = meta[1]
    for j, ref in enumerate(refs[:-1]):
        out[:, pl.ds(pl.multiple_of((chip ^ j) * lanes, lanes), lanes)] = ref[...].astype(F32)


def call(kernel, out_shape, args, scratch=(), flops=0, smem=0):
    specs = [pl.BlockSpec(memory_space=pltpu.SMEM)] * smem
    specs += [pl.BlockSpec(memory_space=pltpu.VMEM)] * (len(args) - smem)
    outs = jax.tree.map(lambda _: pl.BlockSpec(memory_space=pltpu.VMEM), out_shape)
    moved = sum(math.prod(a.shape) * a.dtype.itemsize for a in list(args) + jax.tree.leaves(out_shape))
    return pl.pallas_call(
        kernel,
        out_shape=out_shape,
        in_specs=specs,
        out_specs=outs,
        scratch_shapes=list(scratch),
        compiler_params=pltpu.CompilerParams(vmem_limit_bytes=VMEM_LIMIT),
        cost_estimate=pl.CostEstimate(flops=flops, bytes_accessed=moved, transcendentals=0),
    )(*args)


def local(waves, partner, pair_count, left_station, right_station, owner):
    sta_count = lax.axis_size("sta")
    tm_count = lax.axis_size("tm")
    comps, stations, seg_local, samples = waves.shape
    freqs = samples // 2
    pairs = left_station.shape[1]
    capacity = 2 * pairs // sta_count
    columns = comps * comps * LAGS
    width = columns // tm_count
    chips = sta_count // 2
    sends = tm_count // 2 - 1
    unit = math.gcd(width, LAGS)
    blocks = -(-(LAGS - unit + width) // LAGS)
    scale = 1.0 / math.sqrt(freqs * seg_local * tm_count)
    dft, high_table, low_table, band, inverse = (jnp.asarray(a) for a in tables(samples, freqs, scale))

    t = lax.axis_index("tm")
    me = lax.axis_index("sta")
    meta = jnp.stack([t, me // 2, me % 2]).astype(jnp.int32)
    listed = jnp.where(jnp.arange(pairs, dtype=jnp.int32)[None, :] < pair_count[0], owner, -1)
    other_listed = lax.ppermute(listed, "sta", xor_pairs(sta_count, 1))

    x = waves.reshape(comps * stations, samples)
    half = x.shape[0] // 2
    grid_flops = 2 * (3 * 2 * freqs * samples * stations + 3 * 4 * freqs * pairs * stations)

    def whitened(records, index):
        shape = jax.ShapeDtypeStruct((comps, 2 * freqs, pairs), F32)
        return call(whiten_kernel, shape, (records, dft, band, inverse, index), flops=grid_flops)

    def gather(offset, x, left, right):
        swap = functools.partial(lax.ppermute, axis_name="tm", perm=xor_pairs(tm_count, 1))
        cross = functools.partial(lax.ppermute, axis_name="sta", perm=xor_pairs(sta_count, offset))
        x_next = swap(x)
        p = cross(x)
        g0 = whitened(x, left)
        pa = cross(x_next[:half])
        pb = swap(p[half:])
        h0 = whitened(p, right)
        g1 = whitened(x_next, left)
        return g0, h0, g1, pa, pb

    branches = [functools.partial(gather, k) for k in range(1, sta_count)]
    g0, h0, g1, pa, pb = lax.switch(partner[0, 0] - 1, branches, x, left_station, right_station)

    scratch = [
        pltpu.VMEM((2 * freqs, pairs), BF16),
        pltpu.VMEM((2 * freqs, pairs), BF16),
        pltpu.VMEM((blocks * LAGS, pairs), F32),
    ]
    lag_flops = 2 * 3 * blocks * LAGS * 2 * freqs * pairs
    sent, h1 = call(
        functools.partial(send_kernel, width, blocks, sends),
        (
            jax.ShapeDtypeStruct((sends, width, pairs), BF16),
            jax.ShapeDtypeStruct((comps, 2 * freqs, pairs), F32),
        ),
        (meta, g0, h0, g1, pa, pb, dft, band, inverse, right_station, high_table, low_table),
        scratch, flops=grid_flops + sends * lag_flops, smem=1,
    )
    received = [
        lax.ppermute(sent[j], "tm", xor_pairs(tm_count, 2 * (j + 1))) for j in range(sends)
    ]
    own = call(
        functools.partial(own_kernel, width, blocks),
        jax.ShapeDtypeStruct((width, pairs), F32),
        (meta, g0, h0, g1, h1, high_table, low_table),
        scratch, flops=lag_flops, smem=1,
    )
    total = call(
        total_kernel, jax.ShapeDtypeStruct((width, pairs), BF16), (own, jnp.stack(received)), flops=width * pairs
    )
    other = lax.ppermute(total, "sta", xor_pairs(sta_count, 1))
    lanes = 2 * capacity
    routed = call(
        functools.partial(route_kernel, sta_count, capacity),
        [jax.ShapeDtypeStruct((width, lanes), BF16)] * chips,
        (meta, total, other, listed, other_listed),
        flops=2 * width * 2 * pairs * chips * lanes, smem=1,
    )
    arrived = [
        routed[j] if j == 0 else lax.ppermute(routed[j], "sta", xor_pairs(sta_count, 2 * j)) for j in range(chips)
    ]
    if lanes % 128 == 0:
        result = call(
            functools.partial(place_kernel, lanes),
            jax.ShapeDtypeStruct((width, sta_count * capacity), F32),
            (meta, *arrived), flops=width * sta_count * capacity, smem=1,
        )
    else:
        order = jnp.bitwise_xor(me // 2, jnp.arange(chips, dtype=jnp.int32))
        result = jnp.take(jnp.stack(arrived), order, axis=0).astype(F32)
        result = jnp.transpose(result, (1, 0, 2)).reshape(width, sta_count * capacity)
    return result.T


def solution(mesh):
    in_specs = (
        P(None, "sta", "tm", None),
        P(),
        P("sta"),
        P("sta", None),
        P("sta", None),
        P("sta", None),
    )
    out_specs = P("sta", "tm")
    return jax.shard_map(local, mesh=mesh, in_specs=in_specs, out_specs=out_specs, check_vma=False)
```

```python
import functools
import math

import jax
import jax.numpy as jnp
import numpy as np
from jax import lax
from jax.experimental import pallas as pl
from jax.experimental.pallas import tpu as pltpu
from jax.sharding import PartitionSpec as P

LAGS = 256
HALF_BAND = 21
EPSILON = 1e-06
F32 = jnp.float32
BF16 = jnp.bfloat16
VMEM_LIMIT = 20 * 1024 * 1024
STEP = 32


def xor_pairs(count, mask):
    return [(i, i ^ mask) for i in range(count)]


def split(x):
    hi = x.astype(BF16)
    return hi, (x - hi.astype(F32)).astype(BF16)


def tables(samples, freqs, scale):
    n = np.arange(samples, dtype=np.int64)
    f = np.arange(freqs, dtype=np.int64)
    step = np.float32(2.0 * math.pi / samples)
    phase = (step * np.mod(f[:, None] * n[None, :], samples).astype(np.float32)).astype(np.float32)
    dft = np.concatenate([np.cos(phase), -np.sin(phase)], axis=0).astype(jnp.bfloat16)
    lag = np.arange(LAGS, dtype=np.int64) - LAGS // 2
    phase = (step * np.mod(lag[:, None] * f[None, :], samples).astype(np.float32)).astype(np.float32)
    table = np.concatenate([np.cos(phase), -np.sin(phase)], axis=1) * np.float32(scale)
    high = table.astype(jnp.bfloat16)
    low = (table - high.astype(np.float32)).astype(jnp.bfloat16)
    near = np.abs(f[:, None] - f[None, :]) <= HALF_BAND
    inverse = (1.0 / (3.0 * near.sum(axis=1))).astype(np.float32)[:, None]
    return dft, high, low, near.astype(jnp.bfloat16), np.broadcast_to(inverse, (freqs, 128)).copy()


def whiten_rows(x, dft, band, inverse, index):
    stations = x.shape[0] // 3
    freqs = band.shape[0]
    spectra = [
        lax.dot_general(
            dft, x[c * stations : (c + 1) * stations], (((1,), (1,)), ((), ())), preferred_element_type=F32
        )
        for c in range(3)
    ]
    amplitude = sum(jnp.sqrt(s[:freqs] * s[:freqs] + s[freqs:] * s[freqs:]) for s in spectra)
    high, low = split(amplitude)
    smooth = jnp.dot(band, high, preferred_element_type=F32) + jnp.dot(band, low, preferred_element_type=F32)
    factor = 1.0 / (smooth * inverse[:, :1] + EPSILON)
    factor = jnp.concatenate([factor, factor], axis=0)
    pick = lax.broadcasted_iota(jnp.int32, (stations, index.shape[1]), 0) == index
    pick = pick.astype(F32).astype(BF16)
    pick = jnp.concatenate([pick, pick], axis=0)
    rows = []
    for s in spectra:
        high, low = split(s * factor)
        rows.append(jnp.dot(jnp.concatenate([high, low], axis=1), pick, preferred_element_type=F32))
    return rows


def whiten_kernel(x, dft, band, inverse, index, out):
    rows = whiten_rows(x[...], dft[...], band[...], inverse[...], index[...])
    for c in range(3):
        out[c] = rows[c]


def cross_rows(lefts, rights, a, c, r, step, real, imag):
    freqs = lefts[0].shape[1] // 2
    for left, right in zip(lefts, rights):
        lr, li = left[a, r : r + step], left[a, freqs + r : freqs + r + step]
        rr, ri = right[c, r : r + step], right[c, freqs + r : freqs + r + step]
        real = real + (lr * rr + li * ri)
        imag = imag + (li * rr - lr * ri)
    return real, imag


def component_pair(first, j):
    ac = jnp.minimum(first + j, 8)
    return ac // 3, ac % 3


def cross_kernel(width, blocks, sends, meta, g0, h0, out):
    freqs = g0.shape[1] // 2
    for k in range(sends):
        first = ((meta[0] ^ (2 * (k + 1))) * width) // LAGS
        for j in range(blocks):
            a, c = component_pair(first, j)
            for r in range(0, freqs, STEP):
                real, imag = cross_rows((g0,), (h0,), a, c, r, STEP, 0.0, 0.0)
                out[k * blocks + j, r : r + STEP] = real
                out[k * blocks + j, freqs + r : freqs + r + STEP] = imag


def lag_block(lefts, rights, base, a, c, high_table, low_table, cross_high, cross_low):
    freqs = lefts[0].shape[1] // 2
    for r in range(0, freqs, STEP):
        real, imag = (0.0, 0.0) if base is None else (base[r : r + STEP], base[freqs + r : freqs + r + STEP])
        real, imag = cross_rows(lefts, rights, a, c, r, STEP, real, imag)
        cross_high[r : r + STEP], cross_low[r : r + STEP] = split(real)
        cross_high[freqs + r : freqs + r + STEP], cross_low[freqs + r : freqs + r + STEP] = split(imag)
    return (
        jnp.dot(high_table[...], cross_high[...], preferred_element_type=F32)
        + jnp.dot(low_table[...], cross_high[...], preferred_element_type=F32)
        + jnp.dot(high_table[...], cross_low[...], preferred_element_type=F32)
    )


def send_first_kernel(
    width, rows, have, sends, meta, x0, g1, xa, xb, dft, band, inverse, index, high_table, low_table,
    out, lagged, h1, cross_high, cross_low,
):
    x = jnp.concatenate([xa[...], xb[...]], axis=0)
    white = whiten_rows(x, dft[...], band[...], inverse[...], index[...])
    for c in range(3):
        h1[c] = white[c]
    blocks = x0.shape[0] // sends
    for k in range(sends):
        start = (meta[0] ^ (2 * (k + 1))) * width
        first = start // LAGS
        for j in range(have):
            a, c = component_pair(first, j)
            lagged[k, j * LAGS : (j + 1) * LAGS] = lag_block(
                (g1,), (h1,), x0.at[k * blocks + j], a, c, high_table, low_table, cross_high, cross_low
            )
        out[k] = lagged[k, pl.ds(pl.multiple_of(start - first * LAGS, 16), rows)].astype(BF16)


def send_rest_kernel(
    width, rows, have, sends, meta, x0, g1, h1, lagged_in, high_table, low_table,
    out, cross_high, cross_low, lagged,
):
    blocks = x0.shape[0] // sends
    for k in range(sends):
        start = (meta[0] ^ (2 * (k + 1))) * width
        first = start // LAGS
        lagged[: have * LAGS] = lagged_in[k]
        for j in range(have, blocks):
            a, c = component_pair(first, j)
            lagged[j * LAGS : (j + 1) * LAGS] = lag_block(
                (g1,), (h1,), x0.at[k * blocks + j], a, c, high_table, low_table, cross_high, cross_low
            )
        out[k] = lagged[pl.ds(pl.multiple_of(start - first * LAGS + rows, 16), width - rows)].astype(BF16)


def own_kernel(
    width, rows, blocks, meta, g0, h0, g1, h1, high_table, low_table, out, rest, cross_high, cross_low, lagged
):
    start = meta[0] * width
    first = start // LAGS
    for j in range(blocks):
        a, c = component_pair(first, j)
        lagged[j * LAGS : (j + 1) * LAGS] = lag_block(
            (g0, g1), (h0, h1), None, a, c, high_table, low_table, cross_high, cross_low
        )
    out[...] = lagged[pl.ds(pl.multiple_of(start - first * LAGS, 16), rows)]
    rest[...] = lagged[pl.ds(pl.multiple_of(start - first * LAGS + rows, 16), width - rows)]


def total_kernel(own, received, out):
    total = own[...]
    for j in range(received.shape[0]):
        total = total + received[j].astype(F32)
    out[...] = total.astype(BF16)


def ranks(owner, blocks):
    pairs = owner.shape[1]
    hits = lax.broadcasted_iota(jnp.int32, (blocks, pairs), 0) == owner
    hits = hits.astype(F32)
    earlier = lax.broadcasted_iota(jnp.int32, (pairs, pairs), 0) < lax.broadcasted_iota(jnp.int32, (pairs, pairs), 1)
    before = jnp.dot(hits.astype(BF16), earlier.astype(F32).astype(BF16), preferred_element_type=F32)
    return jnp.sum(before * hits, axis=0, keepdims=True).astype(jnp.int32)


def pick_kernel(blocks, capacity, meta, owner, other_owner, out):
    chip, core = meta[1], meta[2]
    pairs = owner.shape[1]
    for place, (value, lists) in enumerate(((owner[...], core), (other_owner[...], 1 - core))):
        slot = ((value // 2) ^ chip) * (2 * capacity) + lists * capacity + ranks(value, blocks)
        mine = jnp.logical_and(value >= 0, value % 2 == core)
        slot = jnp.where(mine, slot, -1)
        slots = lax.broadcasted_iota(jnp.int32, (blocks * capacity, pairs), 0)
        out[:, place * pairs : (place + 1) * pairs] = (slots == slot).astype(F32).astype(BF16)


def route_kernel(total, other, pick, *outs):
    values = jnp.concatenate([total[...], other[...]], axis=1)
    routed = lax.dot_general(values, pick[...], (((1,), (1,)), ((), ())), preferred_element_type=F32)
    lanes = routed.shape[1] // len(outs)
    for j, out in enumerate(outs):
        out[...] = routed[:, j * lanes : (j + 1) * lanes].astype(BF16)


def place_kernel(lanes, chips, meta, *refs):
    out = refs[-1]
    chip = meta[1]
    for i, ref in enumerate(refs[:-1]):
        first = 0 if i < chips else refs[0].shape[0]
        at = pl.ds(pl.multiple_of((chip ^ (i % chips)) * lanes, lanes), lanes)
        out[first : first + ref.shape[0], at] = ref[...].astype(F32)


def call(kernel, out_shape, args, scratch=(), flops=0, smem=0):
    specs = [pl.BlockSpec(memory_space=pltpu.SMEM)] * smem
    specs += [pl.BlockSpec(memory_space=pltpu.VMEM)] * (len(args) - smem)
    outs = jax.tree.map(lambda _: pl.BlockSpec(memory_space=pltpu.VMEM), out_shape)
    moved = sum(math.prod(a.shape) * a.dtype.itemsize for a in list(args) + jax.tree.leaves(out_shape))
    return pl.pallas_call(
        kernel,
        out_shape=out_shape,
        in_specs=specs,
        out_specs=outs,
        scratch_shapes=list(scratch),
        compiler_params=pltpu.CompilerParams(vmem_limit_bytes=VMEM_LIMIT),
        cost_estimate=pl.CostEstimate(flops=1024, bytes_accessed=1024, transcendentals=0),
    )(*args)


def local(waves, partner, pair_count, left_station, right_station, owner):
    sta_count = lax.axis_size("sta")
    tm_count = lax.axis_size("tm")
    comps, stations, seg_local, samples = waves.shape
    freqs = samples // 2
    pairs = left_station.shape[1]
    capacity = 2 * pairs // sta_count
    width = comps * comps * LAGS // tm_count
    chips = sta_count // 2
    sends = tm_count // 2 - 1
    top = LAGS - math.gcd(width, LAGS)
    blocks = -(-(top + width) // LAGS)
    rows = -(-width // 48) * 16
    have = -(-(top + rows) // LAGS)
    scale = 1.0 / math.sqrt(freqs * seg_local * tm_count)
    dft, high_table, low_table, band, inverse = (jnp.asarray(a) for a in tables(samples, freqs, scale))

    t = lax.axis_index("tm")
    me = lax.axis_index("sta")
    meta = jnp.stack([t, me // 2, me % 2]).astype(jnp.int32)
    x = waves.reshape(comps * stations, samples)
    by_cross = -(-x.shape[0] * 5 // 8 // 16) * 16
    whiten_flops = 2 * (3 * 2 * freqs * samples * stations + 3 * 4 * freqs * pairs * stations)
    rows_shape = jax.ShapeDtypeStruct((comps, 2 * freqs, pairs), F32)

    def whitened(records, index):
        return call(whiten_kernel, rows_shape, (records, dft, band, inverse, index), flops=whiten_flops)

    def gather(offset, meta, x, left, right, owner, pair_count):
        swap = functools.partial(lax.ppermute, axis_name="tm", perm=xor_pairs(tm_count, 1))
        cross = functools.partial(lax.ppermute, axis_name="sta", perm=xor_pairs(sta_count, offset))
        x_next = swap(x)
        p = cross(x)
        g0 = whitened(x, left)
        listed = jnp.where(jnp.arange(pairs, dtype=jnp.int32)[None, :] < pair_count[0], owner, -1)
        other_listed = lax.ppermute(listed, "sta", xor_pairs(sta_count, 1))
        pick = call(
            functools.partial(pick_kernel, sta_count, capacity),
            jax.ShapeDtypeStruct((sta_count * capacity, 2 * pairs), BF16),
            (meta, listed, other_listed), flops=4 * sta_count * pairs * pairs, smem=1,
        )
        near, g0, pick = lax.optimization_barrier((x_next[:by_cross], g0, pick))
        pa = cross(near)
        pb = cross(x_next[by_cross:]) if offset == 1 else swap(p[by_cross:])
        h0 = whitened(p, right)
        g1 = whitened(x_next, left)
        x0 = call(
            functools.partial(cross_kernel, width, blocks, sends),
            jax.ShapeDtypeStruct((sends * blocks, 2 * freqs, pairs), F32),
            (meta, g0, h0), flops=sends * blocks * 8 * freqs * pairs, smem=1,
        )
        return x0, g0, h0, g1, pa, pb, pick

    branches = [functools.partial(gather, k) for k in range(1, sta_count)]
    x0, g0, h0, g1, pa, pb, pick = lax.switch(
        partner[0, 0] - 1, branches, meta, x, left_station, right_station, owner, pair_count
    )

    bands = [pltpu.VMEM((2 * freqs, pairs), BF16)] * 2
    scratch = bands + [pltpu.VMEM((blocks * LAGS, pairs), F32)]
    lag_flops = 2 * 3 * LAGS * 2 * freqs * pairs
    first, lagged, h1 = call(
        functools.partial(send_first_kernel, width, rows, have, sends),
        (
            jax.ShapeDtypeStruct((sends, rows, pairs), BF16),
            jax.ShapeDtypeStruct((sends, have * LAGS, pairs), F32),
            rows_shape,
        ),
        (meta, x0, g1, pa, pb, dft, band, inverse, right_station, high_table, low_table),
        bands, flops=whiten_flops + sends * have * lag_flops, smem=1,
    )
    rest = call(
        functools.partial(send_rest_kernel, width, rows, have, sends),
        jax.ShapeDtypeStruct((sends, width - rows, pairs), BF16),
        (meta, x0, g1, h1, lagged, high_table, low_table),
        scratch, flops=sends * (blocks - have) * lag_flops, smem=1,
    )
    own = call(
        functools.partial(own_kernel, width, rows, blocks),
        (jax.ShapeDtypeStruct((rows, pairs), F32), jax.ShapeDtypeStruct((width - rows, pairs), F32)),
        (meta, g0, h0, g1, h1, high_table, low_table),
        scratch, flops=blocks * lag_flops, smem=1,
    )
    lanes = 2 * capacity
    arrived = []
    routed = None
    for part, mine in zip((first, rest), own):
        if routed is not None:
            mine, *arrived = lax.optimization_barrier((mine, *arrived))
        received = [lax.ppermute(part[j], "tm", xor_pairs(tm_count, 2 * (j + 1))) for j in range(sends)]
        size = mine.shape[0]
        total = call(
            total_kernel, jax.ShapeDtypeStruct((size, pairs), BF16), (mine, jnp.stack(received)), flops=size * pairs
        )
        other = lax.ppermute(total, "sta", xor_pairs(sta_count, 1))
        routed = call(
            route_kernel,
            [jax.ShapeDtypeStruct((size, lanes), BF16)] * chips,
            (total, other, pick),
            flops=2 * size * 2 * pairs * chips * lanes,
        )
        moved = [lax.ppermute(routed[j], "sta", xor_pairs(sta_count, 2 * j)) for j in range(chips - 1, 0, -1)]
        arrived += [routed[0]] + moved[::-1]
    if lanes % 128 == 0:
        result = call(
            functools.partial(place_kernel, lanes, chips),
            jax.ShapeDtypeStruct((width, sta_count * capacity), F32),
            (meta, *arrived), flops=width * sta_count * capacity, smem=1,
        )
    else:
        order = jnp.bitwise_xor(me // 2, jnp.arange(chips, dtype=jnp.int32))
        parts = []
        for part in (arrived[:chips], arrived[chips:]):
            part = jnp.take(jnp.stack(part), order, axis=0).astype(F32)
            parts.append(jnp.transpose(part, (1, 0, 2)).reshape(part.shape[1], sta_count * capacity))
        result = jnp.concatenate(parts, axis=0)
    return result.T


def solution(mesh):
    in_specs = (
        P(None, "sta", "tm", None),
        P(),
        P("sta"),
        P("sta", None),
        P("sta", None),
        P("sta", None),
    )
    out_specs = P("sta", "tm")
    return jax.shard_map(local, mesh=mesh, in_specs=in_specs, out_specs=out_specs, check_vma=False)
```

```python
import functools
import math

import jax
import jax.numpy as jnp
import numpy as np
from jax import lax
from jax.experimental import pallas as pl
from jax.experimental.pallas import tpu as pltpu
from jax.sharding import PartitionSpec as P

LAGS = 256
HALF_BAND = 21
EPSILON = 1e-06
F32 = jnp.float32
BF16 = jnp.bfloat16
VMEM_LIMIT = 14 * 1024 * 1024
STEP = 32


def xor_pairs(count, mask):
    return [(i, i ^ mask) for i in range(count)]


def split(x):
    hi = x.astype(BF16)
    return hi, (x - hi.astype(F32)).astype(BF16)


def tables(samples, freqs, scale):
    n = np.arange(samples, dtype=np.int64)
    f = np.arange(freqs, dtype=np.int64)
    step = np.float32(2.0 * math.pi / samples)
    phase = (step * np.mod(f[:, None] * n[None, :], samples).astype(np.float32)).astype(np.float32)
    dft = np.concatenate([np.cos(phase), -np.sin(phase)], axis=0).astype(jnp.bfloat16)
    lag = np.arange(LAGS, dtype=np.int64) - LAGS // 2
    phase = (step * np.mod(lag[:, None] * f[None, :], samples).astype(np.float32)).astype(np.float32)
    table = np.concatenate([np.cos(phase), -np.sin(phase)], axis=1) * np.float32(scale)
    high = table.astype(jnp.bfloat16)
    low = (table - high.astype(np.float32)).astype(jnp.bfloat16)
    near = np.abs(f[:, None] - f[None, :]) <= HALF_BAND
    inverse = (1.0 / (3.0 * near.sum(axis=1))).astype(np.float32)[:, None]
    return dft, high, low, near.astype(jnp.bfloat16), np.broadcast_to(inverse, (freqs, 128)).copy()


def whiten_factor(amplitude, band, inverse):
    high, low = split(amplitude)
    smooth = jnp.dot(band, high, preferred_element_type=F32) + jnp.dot(band, low, preferred_element_type=F32)
    return 1.0 / (smooth * inverse[:, :1] + EPSILON)


def one_hot(index, stations):
    pick = lax.broadcasted_iota(jnp.int32, (stations, index.shape[1]), 0) == index
    pick = pick.astype(F32).astype(BF16)
    return jnp.concatenate([pick, pick], axis=0)


def whiten_rows(x, dft, band, inverse, index):
    stations = x.shape[0] // 3
    freqs = band.shape[0]
    spectra = lax.dot_general(dft, x, (((1,), (1,)), ((), ())), preferred_element_type=F32)
    spectra = [spectra[:, c * stations : (c + 1) * stations] for c in range(3)]
    amplitude = sum(jnp.sqrt(s[:freqs] * s[:freqs] + s[freqs:] * s[freqs:]) for s in spectra)
    factor = whiten_factor(amplitude, band, inverse)
    factor = jnp.concatenate([factor, factor], axis=0)
    pick = one_hot(index, stations)
    rows = []
    for s in spectra:
        high, low = split(s * factor)
        rows.append(jnp.dot(jnp.concatenate([high, low], axis=1), pick, preferred_element_type=F32))
    return rows


def whiten_kernel(x, dft, band, inverse, index, out, spectra):
    stations = x.shape[0] // 3
    freqs = band.shape[0]

    def transform(c, amplitude):
        at = pl.ds(pl.multiple_of(c * stations, stations), stations)
        s = lax.dot_general(dft[...], x[at], (((1,), (1,)), ((), ())), preferred_element_type=F32)
        spectra[c] = s
        return amplitude + jnp.sqrt(s[:freqs] * s[:freqs] + s[freqs:] * s[freqs:])

    amplitude = lax.fori_loop(0, 3, transform, jnp.zeros((freqs, stations), F32))
    factor = whiten_factor(amplitude, band[...], inverse[...])
    factor = jnp.concatenate([factor, factor], axis=0)
    pick = one_hot(index[...], stations)

    def gather(c, carry):
        high, low = split(spectra[c] * factor)
        out[c] = jnp.dot(jnp.concatenate([high, low], axis=1), pick, preferred_element_type=F32)
        return carry

    lax.fori_loop(0, 3, gather, 0)


def cross_rows(lefts, rights, a, c, r, real, imag):
    freqs = lefts[0].shape[1] // 2
    near, far = pl.ds(r, STEP), pl.ds(freqs + r, STEP)
    for left, right in zip(lefts, rights):
        lr, li = left[a, near], left[a, far]
        rr, ri = right[c, near], right[c, far]
        real = real + (lr * rr + li * ri)
        imag = imag + (li * rr - lr * ri)
    return real, imag


def component_pair(first, j):
    ac = jnp.minimum(first + j, 8)
    return ac // 3, ac % 3


def over_rows(freqs, body):
    def step(i, carry):
        body(pl.multiple_of(i * STEP, STEP))
        return carry

    lax.fori_loop(0, freqs // STEP, step, 0)


def cross_kernel(width, blocks, sends, g0, h0, out):
    freqs = g0.shape[1] // 2

    def block(i, carry):
        first = ((lax.axis_index("tm") ^ (2 * (i // blocks + 1))) * width) // LAGS
        a, c = component_pair(first, i % blocks)

        def rows(r):
            real, imag = cross_rows((g0,), (h0,), a, c, r, 0.0, 0.0)
            out[i, pl.ds(r, STEP)] = real
            out[i, pl.ds(freqs + r, STEP)] = imag

        over_rows(freqs, rows)
        return carry

    lax.fori_loop(0, sends * blocks, block, 0)


def lag_block(lefts, rights, base, a, c, high_table, low_table, cross_high, cross_low):
    freqs = lefts[0].shape[1] // 2

    def rows(r):
        near, far = pl.ds(r, STEP), pl.ds(freqs + r, STEP)
        real, imag = (0.0, 0.0) if base is None else (base[near], base[far])
        real, imag = cross_rows(lefts, rights, a, c, r, real, imag)
        cross_high[near], cross_low[near] = split(real)
        cross_high[far], cross_low[far] = split(imag)

    over_rows(freqs, rows)
    return (
        jnp.dot(high_table[...], cross_high[...], preferred_element_type=F32)
        + jnp.dot(low_table[...], cross_high[...], preferred_element_type=F32)
        + jnp.dot(high_table[...], cross_low[...], preferred_element_type=F32)
    )


def piece(k_piece, width, blocks, lefts, rights, base, lagged, high_table, low_table, cross_high, cross_low):
    start = k_piece * width
    first = start // LAGS

    def block(j, carry):
        a, c = component_pair(first, j)
        lagged[pl.ds(pl.multiple_of(j * LAGS, LAGS), LAGS)] = lag_block(
            lefts, rights, None if base is None else base.at[j], a, c, high_table, low_table, cross_high, cross_low
        )
        return carry

    lax.fori_loop(0, blocks, block, 0)
    return start - first * LAGS


def send_kernel(
    width, blocks, sends, x0, g1, xa, xb, dft, band, inverse, index, high_table, low_table,
    out, rest, h1, cross_high, cross_low, lagged,
):
    x = jnp.concatenate([xa[...], xb[...]], axis=0)
    white = whiten_rows(x, dft[...], band[...], inverse[...], index[...])
    for c in range(3):
        h1[c] = white[c]
    rows = out.shape[1]
    for k in range(sends):
        base = x0.at[k * blocks : (k + 1) * blocks]
        shift = piece(
            lax.axis_index("tm") ^ (2 * (k + 1)), width, blocks, (g1,), (h1,), base, lagged,
            high_table, low_table, cross_high, cross_low,
        )
        out[k] = lagged[pl.ds(pl.multiple_of(shift, 16), rows)].astype(BF16)
        rest[k] = lagged[pl.ds(pl.multiple_of(shift + rows, 16), width - rows)].astype(BF16)


def own_kernel(
    width, blocks, g0, h0, g1, h1, high_table, low_table, out, rest, cross_high, cross_low, lagged
):
    shift = piece(
        lax.axis_index("tm"), width, blocks, (g0, g1), (h0, h1), None, lagged, high_table, low_table, cross_high, cross_low
    )
    rows = out.shape[0]
    out[...] = lagged[pl.ds(pl.multiple_of(shift, 16), rows)]
    rest[...] = lagged[pl.ds(pl.multiple_of(shift + rows, 16), width - rows)]


def total_kernel(own, received, out):
    total = own[...]
    for j in range(received.shape[0]):
        total = total + received[j].astype(F32)
    out[...] = total.astype(BF16)


def ranks(owner, blocks):
    pairs = owner.shape[1]
    hits = lax.broadcasted_iota(jnp.int32, (blocks, pairs), 0) == owner
    hits = hits.astype(F32)
    earlier = lax.broadcasted_iota(jnp.int32, (pairs, pairs), 0) < lax.broadcasted_iota(jnp.int32, (pairs, pairs), 1)
    before = jnp.dot(hits.astype(BF16), earlier.astype(F32).astype(BF16), preferred_element_type=F32)
    return jnp.sum(before * hits, axis=0, keepdims=True).astype(jnp.int32)


def pick_kernel(blocks, capacity, owner, other_owner, out):
    me = lax.axis_index("sta")
    chip, core = me // 2, me % 2
    pairs = owner.shape[1]
    for place, (value, lists) in enumerate(((owner[...], core), (other_owner[...], 1 - core))):
        slot = ((value // 2) ^ chip) * (2 * capacity) + lists * capacity + ranks(value, blocks)
        mine = jnp.logical_and(value >= 0, value % 2 == core)
        slot = jnp.where(mine, slot, -1)
        slots = lax.broadcasted_iota(jnp.int32, (blocks * capacity, pairs), 0)
        out[:, place * pairs : (place + 1) * pairs] = (slots == slot).astype(F32).astype(BF16)


def route_kernel(total, other, pick, *outs):
    values = jnp.concatenate([total[...], other[...]], axis=1)
    routed = lax.dot_general(values, pick[...], (((1,), (1,)), ((), ())), preferred_element_type=F32)
    lanes = routed.shape[1] // len(outs)
    for j, out in enumerate(outs):
        out[...] = routed[:, j * lanes : (j + 1) * lanes].astype(BF16)


def place_kernel(lanes, top, *refs):
    out, rows, sems = refs[-3:]
    chip = lax.axis_index("sta") // 2
    copies = []
    for j in range(rows.shape[0]):
        at = pl.ds(pl.multiple_of((chip ^ j) * lanes, lanes), lanes)
        rows[j] = refs[j][...].astype(F32)
        copies.append(pltpu.make_async_copy(rows.at[j], out.at[pl.ds(top, rows.shape[1]), at], sems.at[j]))
        copies[-1].start()
    for copy in copies:
        copy.wait()


def place(lanes, top, shape, arrived, before):
    chips = len(arrived)
    args = list(arrived) + ([] if before is None else [before])
    anywhere = pl.BlockSpec(memory_space=pl.ANY)
    return pl.pallas_call(
        functools.partial(place_kernel, lanes, top),
        out_shape=shape,
        in_specs=[pl.BlockSpec(memory_space=pltpu.VMEM)] * chips + [anywhere] * (before is not None),
        out_specs=anywhere,
        scratch_shapes=[pltpu.VMEM((chips, arrived[0].shape[0], lanes), F32), pltpu.SemaphoreType.DMA((chips,))],
        input_output_aliases={} if before is None else {chips: 0},
        compiler_params=pltpu.CompilerParams(vmem_limit_bytes=VMEM_LIMIT),
        cost_estimate=pl.CostEstimate(flops=1024, bytes_accessed=1024, transcendentals=0),
    )(*args)


def call(kernel, out_shape, args, scratch=()):
    outs = jax.tree.map(lambda _: pl.BlockSpec(memory_space=pltpu.VMEM), out_shape)
    return pl.pallas_call(
        kernel,
        out_shape=out_shape,
        in_specs=[pl.BlockSpec(memory_space=pltpu.VMEM)] * len(args),
        out_specs=outs,
        scratch_shapes=list(scratch),
        compiler_params=pltpu.CompilerParams(vmem_limit_bytes=VMEM_LIMIT),
        cost_estimate=pl.CostEstimate(flops=1024, bytes_accessed=1024, transcendentals=0),
    )(*args)


def local(waves, partner, pair_count, left_station, right_station, owner):
    sta_count = lax.axis_size("sta")
    tm_count = lax.axis_size("tm")
    comps, stations, seg_local, samples = waves.shape
    freqs = samples // 2
    pairs = left_station.shape[1]
    capacity = 2 * pairs // sta_count
    width = comps * comps * LAGS // tm_count
    chips = sta_count // 2
    sends = tm_count // 2 - 1
    top = LAGS - math.gcd(width, LAGS)
    blocks = -(-(top + width) // LAGS)
    rows = -(-width // 48) * 16
    scale = 1.0 / math.sqrt(freqs * seg_local * tm_count)
    dft, high_table, low_table, band, inverse = (jnp.asarray(a) for a in tables(samples, freqs, scale))

    x = waves.reshape(comps * stations, samples)
    by_cross = -(-x.shape[0] * 5 // 8 // 16) * 16
    rows_shape = jax.ShapeDtypeStruct((comps, 2 * freqs, pairs), F32)

    def whitened(records, index):
        return call(
            whiten_kernel, rows_shape, (records, dft, band, inverse, index),
            [pltpu.VMEM((comps, 2 * freqs, stations), F32)],
        )

    def gather(offset, x, left, right, owner, pair_count):
        swap = functools.partial(lax.ppermute, axis_name="tm", perm=xor_pairs(tm_count, 1))
        cross = functools.partial(lax.ppermute, axis_name="sta", perm=xor_pairs(sta_count, offset))
        p = cross(x)
        x_next = swap(x)
        g0 = whitened(x, left)
        listed = jnp.where(jnp.arange(pairs, dtype=jnp.int32)[None, :] < pair_count[0], owner, -1)
        other_listed = lax.ppermute(listed, "sta", xor_pairs(sta_count, 1))
        pick = call(
            functools.partial(pick_kernel, sta_count, capacity),
            jax.ShapeDtypeStruct((sta_count * capacity, 2 * pairs), BF16),
            (listed, other_listed),
        )
        near, g0, pick = lax.optimization_barrier((x_next[:by_cross], g0, pick))
        pa = cross(near)
        pb = cross(x_next[by_cross:]) if offset == 1 else swap(p[by_cross:])
        g1 = whitened(x_next, left)
        p, g1 = lax.optimization_barrier((p, g1))
        h0 = whitened(p, right)
        x0 = call(
            functools.partial(cross_kernel, width, blocks, sends),
            jax.ShapeDtypeStruct((sends * blocks, 2 * freqs, pairs), F32),
            (g0, h0),
        )
        first, rest, h1 = call(
            functools.partial(send_kernel, width, blocks, sends),
            (
                jax.ShapeDtypeStruct((sends, rows, pairs), BF16),
                jax.ShapeDtypeStruct((sends, width - rows, pairs), BF16),
                rows_shape,
            ),
            (x0, g1, pa, pb, dft, band, inverse, right, high_table, low_table),
            scratch,
        )
        received = exchange(first)
        own = call(
            functools.partial(own_kernel, width, blocks),
            (jax.ShapeDtypeStruct((rows, pairs), F32), jax.ShapeDtypeStruct((width - rows, pairs), F32)),
            (g0, h0, g1, h1, high_table, low_table),
            scratch,
        )
        return received, rest, own, pick

    def exchange(part):
        return [lax.ppermute(part[j], "tm", xor_pairs(tm_count, 2 * (j + 1))) for j in range(sends)]

    scratch = [pltpu.VMEM((2 * freqs, pairs), BF16)] * 2 + [pltpu.VMEM((blocks * LAGS, pairs), F32)]
    branches = [functools.partial(gather, k) for k in range(1, sta_count)]
    received, rest, own, pick = lax.switch(
        partner[0, 0] - 1, branches, x, left_station, right_station, owner, pair_count
    )
    received = [received, exchange(rest)]
    lanes = 2 * capacity
    shape = jax.ShapeDtypeStruct((width, sta_count * capacity), F32)
    parts, arrived, result = [], [], None
    for got, mine in zip(received, own):
        mine = lax.optimization_barrier((mine, *arrived))[0]
        size = mine.shape[0]
        total = call(total_kernel, jax.ShapeDtypeStruct((size, pairs), BF16), (mine, jnp.stack(got)))
        other = lax.ppermute(total, "sta", xor_pairs(sta_count, 1))
        routed = call(route_kernel, [jax.ShapeDtypeStruct((size, lanes), BF16)] * chips, (total, other, pick))
        arrived = [lax.ppermute(routed[j], "sta", xor_pairs(sta_count, 2 * j)) for j in range(chips - 1, 0, -1)]
        arrived = [routed[0]] + arrived[::-1]
        if lanes % 128 == 0:
            result = place(lanes, 0 if result is None else rows, shape, arrived, result)
        else:
            order = jnp.bitwise_xor(lax.axis_index("sta") // 2, jnp.arange(chips, dtype=jnp.int32))
            arrived = jnp.take(jnp.stack(arrived), order, axis=0).astype(F32)
            parts.append(jnp.transpose(arrived, (1, 0, 2)).reshape(size, sta_count * capacity))
            result = jnp.concatenate(parts, axis=0)
    return result.T


def solution(mesh):
    in_specs = (
        P(None, "sta", "tm", None),
        P(),
        P("sta"),
        P("sta", None),
        P("sta", None),
        P("sta", None),
    )
    out_specs = P("sta", "tm")
    return jax.shard_map(local, mesh=mesh, in_specs=in_specs, out_specs=out_specs, check_vma=False)
```

```python
import functools
import math

import jax
import jax.numpy as jnp
import numpy as np
from jax import lax
from jax.experimental import pallas as pl
from jax.experimental.pallas import tpu as pltpu
from jax.sharding import PartitionSpec as P

LAGS = 256
HALF_BAND = 21
EPSILON = 1e-06
F32 = jnp.float32
BF16 = jnp.bfloat16
VMEM_LIMIT = 14 * 1024 * 1024
STEP = 32


def xor_pairs(count, mask):
    return [(i, i ^ mask) for i in range(count)]


def split(x):
    hi = x.astype(BF16)
    return hi, (x - hi.astype(F32)).astype(BF16)


def tables(samples, freqs, scale):
    n = np.arange(samples, dtype=np.int64)
    f = np.arange(freqs, dtype=np.int64)
    step = np.float32(2.0 * math.pi / samples)
    phase = (step * np.mod(f[:, None] * n[None, :], samples).astype(np.float32)).astype(np.float32)
    dft = np.concatenate([np.cos(phase), -np.sin(phase)], axis=0).astype(jnp.bfloat16)
    lag = np.arange(LAGS, dtype=np.int64) - LAGS // 2
    phase = (step * np.mod(lag[:, None] * f[None, :], samples).astype(np.float32)).astype(np.float32)
    table = np.concatenate([np.cos(phase), -np.sin(phase)], axis=1) * np.float32(scale)
    high = table.astype(jnp.bfloat16)
    low = (table - high.astype(np.float32)).astype(jnp.bfloat16)
    near = np.abs(f[:, None] - f[None, :]) <= HALF_BAND
    inverse = (1.0 / (3.0 * near.sum(axis=1))).astype(np.float32)[:, None]
    return dft, high, low, near.astype(jnp.bfloat16), np.broadcast_to(inverse, (freqs, 128)).copy()


def whiten_factor(amplitude, band, inverse):
    high, low = split(amplitude)
    smooth = jnp.dot(band, high, preferred_element_type=F32) + jnp.dot(band, low, preferred_element_type=F32)
    return 1.0 / (smooth * inverse[:, :1] + EPSILON)


def one_hot(index, stations):
    pick = lax.broadcasted_iota(jnp.int32, (stations, index.shape[1]), 0) == index
    pick = pick.astype(F32).astype(BF16)
    return jnp.concatenate([pick, pick], axis=0)


def whiten_rows(x, dft, band, inverse, index):
    stations = x.shape[0] // 3
    freqs = band.shape[0]
    spectra = lax.dot_general(dft, x, (((1,), (1,)), ((), ())), preferred_element_type=F32)
    spectra = [spectra[:, c * stations : (c + 1) * stations] for c in range(3)]
    amplitude = sum(jnp.sqrt(s[:freqs] * s[:freqs] + s[freqs:] * s[freqs:]) for s in spectra)
    factor = whiten_factor(amplitude, band, inverse)
    factor = jnp.concatenate([factor, factor], axis=0)
    pick = one_hot(index, stations)
    rows = []
    for s in spectra:
        high, low = split(s * factor)
        rows.append(jnp.dot(jnp.concatenate([high, low], axis=1), pick, preferred_element_type=F32))
    return rows


def whiten_kernel(x, dft, band, inverse, index, out, spectra):
    stations = x.shape[0] // 3
    freqs = band.shape[0]

    def transform(c, amplitude):
        at = pl.ds(pl.multiple_of(c * stations, stations), stations)
        s = lax.dot_general(dft[...], x[at], (((1,), (1,)), ((), ())), preferred_element_type=F32)
        spectra[c] = s
        return amplitude + jnp.sqrt(s[:freqs] * s[:freqs] + s[freqs:] * s[freqs:])

    amplitude = lax.fori_loop(0, 3, transform, jnp.zeros((freqs, stations), F32))
    factor = whiten_factor(amplitude, band[...], inverse[...])
    factor = jnp.concatenate([factor, factor], axis=0)
    pick = one_hot(index[...], stations)

    def gather(c, carry):
        high, low = split(spectra[c] * factor)
        out[c] = jnp.dot(jnp.concatenate([high, low], axis=1), pick, preferred_element_type=F32)
        return carry

    lax.fori_loop(0, 3, gather, 0)


def cross_rows(lefts, rights, a, c, r, real, imag):
    freqs = lefts[0].shape[1] // 2
    near, far = pl.ds(r, STEP), pl.ds(freqs + r, STEP)
    for left, right in zip(lefts, rights):
        lr, li = left[a, near], left[a, far]
        rr, ri = right[c, near], right[c, far]
        real = real + (lr * rr + li * ri)
        imag = imag + (li * rr - lr * ri)
    return real, imag


def component_pair(first, j):
    ac = jnp.minimum(first + j, 8)
    return ac // 3, ac % 3


def over(count, size, body, unrolled=False):
    if unrolled:
        for i in range(count):
            body(i, i * size)
        return

    def step(i, carry):
        body(i, pl.multiple_of(i * size, size))
        return carry

    lax.fori_loop(0, count, step, 0)


def cross_kernel(width, blocks, sends, g0, h0, out):
    freqs = g0.shape[1] // 2

    def block(i, carry):
        first = ((lax.axis_index("tm") ^ (2 * (i // blocks + 1))) * width) // LAGS
        a, c = component_pair(first, i % blocks)

        def rows(_, r):
            real, imag = cross_rows((g0,), (h0,), a, c, r, 0.0, 0.0)
            out[i, pl.ds(r, STEP)] = real
            out[i, pl.ds(freqs + r, STEP)] = imag

        over(freqs // STEP, STEP, rows)
        return carry

    lax.fori_loop(0, sends * blocks, block, 0)


def lag_block(lefts, rights, base, a, c, high_table, low_table, cross_high, cross_low, unrolled):
    freqs = lefts[0].shape[1] // 2

    def rows(_, r):
        near, far = pl.ds(r, STEP), pl.ds(freqs + r, STEP)
        real, imag = (0.0, 0.0) if base is None else (base[near], base[far])
        real, imag = cross_rows(lefts, rights, a, c, r, real, imag)
        cross_high[near], cross_low[near] = split(real)
        cross_high[far], cross_low[far] = split(imag)

    over(freqs // STEP, STEP, rows, unrolled)
    return (
        jnp.dot(high_table[...], cross_high[...], preferred_element_type=F32)
        + jnp.dot(low_table[...], cross_high[...], preferred_element_type=F32)
        + jnp.dot(high_table[...], cross_low[...], preferred_element_type=F32)
    )


def piece(
    number, width, blocks, lefts, rights, base, lagged, high_table, low_table, cross_high, cross_low, unrolled
):
    start = number * width
    first = start // LAGS

    def block(j, row):
        a, c = component_pair(first, j)
        lagged[pl.ds(row, LAGS)] = lag_block(
            lefts, rights, None if base is None else base.at[j], a, c,
            high_table, low_table, cross_high, cross_low, unrolled,
        )

    over(blocks, LAGS, block, unrolled)
    return start - first * LAGS


def send_kernel(
    width, blocks, sends, x0, g1, xa, xb, dft, band, inverse, index, high_table, low_table,
    out, rest, h1, cross_high, cross_low, lagged,
):
    x = jnp.concatenate([xa[...], xb[...]], axis=0)
    white = whiten_rows(x, dft[...], band[...], inverse[...], index[...])
    for c in range(3):
        h1[c] = white[c]
    rows = out.shape[1]
    for k in range(sends):
        base = x0.at[k * blocks : (k + 1) * blocks]
        shift = piece(
            lax.axis_index("tm") ^ (2 * (k + 1)), width, blocks, (g1,), (h1,), base, lagged,
            high_table, low_table, cross_high, cross_low, sends == 1,
        )
        out[k] = lagged[pl.ds(pl.multiple_of(shift, 16), rows)].astype(BF16)
        rest[k] = lagged[pl.ds(pl.multiple_of(shift + rows, 16), width - rows)].astype(BF16)


def own_kernel(
    width, blocks, g0, h0, g1, h1, high_table, low_table, out, rest, cross_high, cross_low, lagged
):
    shift = piece(
        lax.axis_index("tm"), width, blocks, (g0, g1), (h0, h1), None, lagged,
        high_table, low_table, cross_high, cross_low, False,
    )
    rows = out.shape[0]
    out[...] = lagged[pl.ds(pl.multiple_of(shift, 16), rows)]
    rest[...] = lagged[pl.ds(pl.multiple_of(shift + rows, 16), width - rows)]


def total_kernel(own, received, out):
    total = own[...]
    for j in range(received.shape[0]):
        total = total + received[j].astype(F32)
    out[...] = total.astype(BF16)


def ranks(owner, blocks):
    pairs = owner.shape[1]
    hits = lax.broadcasted_iota(jnp.int32, (blocks, pairs), 0) == owner
    hits = hits.astype(F32)
    earlier = lax.broadcasted_iota(jnp.int32, (pairs, pairs), 0) < lax.broadcasted_iota(jnp.int32, (pairs, pairs), 1)
    before = jnp.dot(hits.astype(BF16), earlier.astype(F32).astype(BF16), preferred_element_type=F32)
    return jnp.sum(before * hits, axis=0, keepdims=True).astype(jnp.int32)


def pick_kernel(blocks, capacity, owner, other_owner, out):
    me = lax.axis_index("sta")
    chip, core = me // 2, me % 2
    pairs = owner.shape[1]
    for place, (value, lists) in enumerate(((owner[...], core), (other_owner[...], 1 - core))):
        slot = ((value // 2) ^ chip) * (2 * capacity) + lists * capacity + ranks(value, blocks)
        mine = jnp.logical_and(value >= 0, value % 2 == core)
        slot = jnp.where(mine, slot, -1)
        slots = lax.broadcasted_iota(jnp.int32, (blocks * capacity, pairs), 0)
        out[:, place * pairs : (place + 1) * pairs] = (slots == slot).astype(F32).astype(BF16)


def route_kernel(total, other, pick, *outs):
    values = jnp.concatenate([total[...], other[...]], axis=1)
    routed = lax.dot_general(values, pick[...], (((1,), (1,)), ((), ())), preferred_element_type=F32)
    lanes = routed.shape[1] // len(outs)
    for j, out in enumerate(outs):
        out[...] = routed[:, j * lanes : (j + 1) * lanes].astype(BF16)


def place_kernel(lanes, top, *refs):
    out, rows, sems = refs[-3:]
    chip = lax.axis_index("sta") // 2
    copies = []
    for j in range(rows.shape[0]):
        at = pl.ds(pl.multiple_of((chip ^ j) * lanes, lanes), lanes)
        rows[j] = refs[j][...].astype(F32)
        copies.append(pltpu.make_async_copy(rows.at[j], out.at[pl.ds(top, rows.shape[1]), at], sems.at[j]))
        copies[-1].start()
    for copy in copies:
        copy.wait()


def place(lanes, top, shape, arrived, before):
    chips = len(arrived)
    args = list(arrived) + ([] if before is None else [before])
    anywhere = pl.BlockSpec(memory_space=pl.ANY)
    return pl.pallas_call(
        functools.partial(place_kernel, lanes, top),
        out_shape=shape,
        in_specs=[pl.BlockSpec(memory_space=pltpu.VMEM)] * chips + [anywhere] * (before is not None),
        out_specs=anywhere,
        scratch_shapes=[pltpu.VMEM((chips, arrived[0].shape[0], lanes), F32), pltpu.SemaphoreType.DMA((chips,))],
        input_output_aliases={} if before is None else {chips: 0},
        compiler_params=pltpu.CompilerParams(vmem_limit_bytes=VMEM_LIMIT),
        cost_estimate=pl.CostEstimate(flops=1024, bytes_accessed=1024, transcendentals=0),
    )(*args)


def call(kernel, out_shape, args, scratch=()):
    outs = jax.tree.map(lambda _: pl.BlockSpec(memory_space=pltpu.VMEM), out_shape)
    return pl.pallas_call(
        kernel,
        out_shape=out_shape,
        in_specs=[pl.BlockSpec(memory_space=pltpu.VMEM)] * len(args),
        out_specs=outs,
        scratch_shapes=list(scratch),
        compiler_params=pltpu.CompilerParams(vmem_limit_bytes=VMEM_LIMIT),
        cost_estimate=pl.CostEstimate(flops=1024, bytes_accessed=1024, transcendentals=0),
    )(*args)


def local(waves, partner, pair_count, left_station, right_station, owner):
    sta_count = lax.axis_size("sta")
    tm_count = lax.axis_size("tm")
    comps, stations, seg_local, samples = waves.shape
    freqs = samples // 2
    pairs = left_station.shape[1]
    capacity = 2 * pairs // sta_count
    width = comps * comps * LAGS // tm_count
    chips = sta_count // 2
    sends = tm_count // 2 - 1
    top = LAGS - math.gcd(width, LAGS)
    blocks = -(-(top + width) // LAGS)
    rows = width * 7 // 144 * 16
    scale = 1.0 / math.sqrt(freqs * seg_local * tm_count)
    dft, high_table, low_table, band, inverse = (jnp.asarray(a) for a in tables(samples, freqs, scale))

    x = waves.reshape(comps * stations, samples)
    by_cross = -(-x.shape[0] * 5 // 8 // 16) * 16
    rows_shape = jax.ShapeDtypeStruct((comps, 2 * freqs, pairs), F32)

    def whitened(records, index):
        return call(
            whiten_kernel, rows_shape, (records, dft, band, inverse, index),
            [pltpu.VMEM((comps, 2 * freqs, stations), F32)],
        )

    def gather(offset, x, left, right, owner, pair_count):
        swap = functools.partial(lax.ppermute, axis_name="tm", perm=xor_pairs(tm_count, 1))
        cross = functools.partial(lax.ppermute, axis_name="sta", perm=xor_pairs(sta_count, offset))
        p = cross(x)
        x_next = swap(x)
        g0 = whitened(x, left)
        listed = jnp.where(jnp.arange(pairs, dtype=jnp.int32)[None, :] < pair_count[0], owner, -1)
        other_listed = lax.ppermute(listed, "sta", xor_pairs(sta_count, 1))
        pick = call(
            functools.partial(pick_kernel, sta_count, capacity),
            jax.ShapeDtypeStruct((sta_count * capacity, 2 * pairs), BF16),
            (listed, other_listed),
        )
        near, g0, pick = lax.optimization_barrier((x_next[:by_cross], g0, pick))
        pa = cross(near)
        pb = cross(x_next[by_cross:]) if offset == 1 else swap(p[by_cross:])
        g1 = whitened(x_next, left)
        p, g1 = lax.optimization_barrier((p, g1))
        h0 = whitened(p, right)
        x0 = call(
            functools.partial(cross_kernel, width, blocks, sends),
            jax.ShapeDtypeStruct((sends * blocks, 2 * freqs, pairs), F32),
            (g0, h0),
        )
        first, rest, h1 = call(
            functools.partial(send_kernel, width, blocks, sends),
            (
                jax.ShapeDtypeStruct((sends, rows, pairs), BF16),
                jax.ShapeDtypeStruct((sends, width - rows, pairs), BF16),
                rows_shape,
            ),
            (x0, g1, pa, pb, dft, band, inverse, right, high_table, low_table),
            scratch,
        )
        received = exchange(first)
        own = call(
            functools.partial(own_kernel, width, blocks),
            (jax.ShapeDtypeStruct((rows, pairs), F32), jax.ShapeDtypeStruct((width - rows, pairs), F32)),
            (g0, h0, g1, h1, high_table, low_table),
            scratch,
        )
        return total(own[0], received), rest, own[1], pick

    def total(mine, received):
        shape = jax.ShapeDtypeStruct(mine.shape, BF16)
        return call(total_kernel, shape, (mine, jnp.stack(received)))

    def exchange(part):
        return [lax.ppermute(part[j], "tm", xor_pairs(tm_count, 2 * (j + 1))) for j in range(sends)]

    scratch = [pltpu.VMEM((2 * freqs, pairs), BF16)] * 2 + [pltpu.VMEM((blocks * LAGS, pairs), F32)]
    branches = [functools.partial(gather, k) for k in range(1, sta_count)]
    first, rest, own, pick = lax.switch(
        partner.reshape(-1)[0] - 1, branches, x, left_station, right_station, owner, pair_count
    )
    second = total(own, exchange(rest))
    lanes = 2 * capacity
    shape = jax.ShapeDtypeStruct((width, sta_count * capacity), F32)
    parts, result = [], None
    for summed in (first, second):
        size = summed.shape[0]
        other = lax.ppermute(summed, "sta", xor_pairs(sta_count, 1))
        routed = call(route_kernel, [jax.ShapeDtypeStruct((size, lanes), BF16)] * chips, (summed, other, pick))
        arrived = [lax.ppermute(routed[j], "sta", xor_pairs(sta_count, 2 * j)) for j in range(chips - 1, 0, -1)]
        arrived = [routed[0]] + arrived[::-1]
        if lanes % 128 == 0:
            result = place(lanes, 0 if result is None else rows, shape, arrived, result)
        else:
            order = jnp.bitwise_xor(lax.axis_index("sta") // 2, jnp.arange(chips, dtype=jnp.int32))
            arrived = jnp.take(jnp.stack(arrived), order, axis=0).astype(F32)
            parts.append(jnp.transpose(arrived, (1, 0, 2)).reshape(size, sta_count * capacity))
            result = jnp.concatenate(parts, axis=0)
    return result.T


def solution(mesh):
    in_specs = (
        P(None, "sta", "tm", None),
        P(),
        P("sta"),
        P("sta", None),
        P("sta", None),
        P("sta", None),
    )
    out_specs = P("sta", "tm")
    return jax.shard_map(local, mesh=mesh, in_specs=in_specs, out_specs=out_specs, check_vma=False)
```

```python
import functools
import math

import jax
import jax.numpy as jnp
import numpy as np
from jax import lax
from jax.experimental import pallas as pl
from jax.experimental.pallas import tpu as pltpu
from jax.sharding import PartitionSpec as P

LAGS = 256
HALF_BAND = 21
EPSILON = 1e-06
F32 = jnp.float32
BF16 = jnp.bfloat16
VMEM_LIMIT = 14 * 1024 * 1024
STEP = 32


def xor_pairs(count, mask):
    return [(i, i ^ mask) for i in range(count)]


def split(x):
    hi = x.astype(BF16)
    return hi, (x - hi.astype(F32)).astype(BF16)


def tables(samples, freqs, scale):
    n = np.arange(samples, dtype=np.int64)
    f = np.arange(freqs, dtype=np.int64)
    step = np.float32(2.0 * math.pi / samples)
    phase = (step * np.mod(f[:, None] * n[None, :], samples).astype(np.float32)).astype(np.float32)
    dft = np.concatenate([np.cos(phase), -np.sin(phase)], axis=0).astype(jnp.bfloat16)
    lag = np.arange(LAGS, dtype=np.int64) - LAGS // 2
    phase = (step * np.mod(lag[:, None] * f[None, :], samples).astype(np.float32)).astype(np.float32)
    table = np.concatenate([np.cos(phase), -np.sin(phase)], axis=1) * np.float32(scale)
    high = table.astype(jnp.bfloat16)
    low = (table - high.astype(np.float32)).astype(jnp.bfloat16)
    near = np.abs(f[:, None] - f[None, :]) <= HALF_BAND
    inverse = (1.0 / (3.0 * near.sum(axis=1))).astype(np.float32)[:, None]
    return dft, high, low, near.astype(jnp.bfloat16), np.broadcast_to(inverse, (freqs, 128)).copy()


def whiten_factor(amplitude, band, inverse):
    high, low = split(amplitude)
    smooth = jnp.dot(band, high, preferred_element_type=F32) + jnp.dot(band, low, preferred_element_type=F32)
    return 1.0 / (smooth * inverse[:, :1] + EPSILON)


def one_hot(index, stations):
    pick = lax.broadcasted_iota(jnp.int32, (stations, index.shape[1]), 0) == index
    pick = pick.astype(F32).astype(BF16)
    return jnp.concatenate([pick, pick], axis=0)


def whiten_rows(x, dft, band, inverse, index):
    stations = x.shape[0] // 3
    freqs = band.shape[0]
    spectra = lax.dot_general(dft, x, (((1,), (1,)), ((), ())), preferred_element_type=F32)
    spectra = [spectra[:, c * stations : (c + 1) * stations] for c in range(3)]
    amplitude = sum(jnp.sqrt(s[:freqs] * s[:freqs] + s[freqs:] * s[freqs:]) for s in spectra)
    factor = whiten_factor(amplitude, band, inverse)
    factor = jnp.concatenate([factor, factor], axis=0)
    pick = one_hot(index, stations)
    rows = []
    for s in spectra:
        high, low = split(s * factor)
        rows.append(jnp.dot(jnp.concatenate([high, low], axis=1), pick, preferred_element_type=F32))
    return rows


def whiten_kernel(x, dft, band, inverse, index, out, spectra):
    stations = x.shape[0] // 3
    freqs = band.shape[0]

    def transform(c, amplitude):
        at = pl.ds(pl.multiple_of(c * stations, stations), stations)
        s = lax.dot_general(dft[...], x[at], (((1,), (1,)), ((), ())), preferred_element_type=F32)
        spectra[c] = s
        return amplitude + jnp.sqrt(s[:freqs] * s[:freqs] + s[freqs:] * s[freqs:])

    amplitude = lax.fori_loop(0, 3, transform, jnp.zeros((freqs, stations), F32))
    factor = whiten_factor(amplitude, band[...], inverse[...])
    factor = jnp.concatenate([factor, factor], axis=0)
    pick = one_hot(index[...], stations)

    def gather(c, carry):
        high, low = split(spectra[c] * factor)
        out[c] = jnp.dot(jnp.concatenate([high, low], axis=1), pick, preferred_element_type=F32)
        return carry

    lax.fori_loop(0, 3, gather, 0)


def cross_rows(lefts, rights, a, c, r, real, imag):
    freqs = lefts[0].shape[1] // 2
    near, far = pl.ds(r, STEP), pl.ds(freqs + r, STEP)
    for left, right in zip(lefts, rights):
        lr, li = left[a, near], left[a, far]
        rr, ri = right[c, near], right[c, far]
        real = real + (lr * rr + li * ri)
        imag = imag + (li * rr - lr * ri)
    return real, imag


def component_pair(first, j):
    ac = jnp.minimum(first + j, 8)
    return ac // 3, ac % 3


def over(count, size, body, unrolled=False):
    if unrolled:
        for i in range(count):
            body(i, i * size)
        return

    def step(i, carry):
        body(i, pl.multiple_of(i * size, size))
        return carry

    lax.fori_loop(0, count, step, 0)


def cross_kernel(width, blocks, sends, g0, h0, out):
    freqs = g0.shape[1] // 2

    def block(i, carry):
        first = ((lax.axis_index("tm") ^ (2 * (i // blocks + 1))) * width) // LAGS
        a, c = component_pair(first, i % blocks)

        def rows(_, r):
            real, imag = cross_rows((g0,), (h0,), a, c, r, 0.0, 0.0)
            out[i, pl.ds(r, STEP)] = real
            out[i, pl.ds(freqs + r, STEP)] = imag

        over(freqs // STEP, STEP, rows)
        return carry

    lax.fori_loop(0, sends * blocks, block, 0)


def lag_block(lefts, rights, base, a, c, high_table, low_table, cross_high, cross_low, unrolled):
    freqs = lefts[0].shape[1] // 2

    def rows(_, r):
        near, far = pl.ds(r, STEP), pl.ds(freqs + r, STEP)
        real, imag = (0.0, 0.0) if base is None else (base[near], base[far])
        real, imag = cross_rows(lefts, rights, a, c, r, real, imag)
        cross_high[near], cross_low[near] = split(real)
        cross_high[far], cross_low[far] = split(imag)

    over(freqs // STEP, STEP, rows, unrolled)
    return (
        jnp.dot(high_table[...], cross_high[...], preferred_element_type=F32)
        + jnp.dot(low_table[...], cross_high[...], preferred_element_type=F32)
        + jnp.dot(high_table[...], cross_low[...], preferred_element_type=F32)
    )


def piece(
    number, width, blocks, lefts, rights, base, lagged, high_table, low_table, cross_high, cross_low, unrolled
):
    start = number * width
    first = start // LAGS

    def block(j, row):
        a, c = component_pair(first, j)
        lagged[pl.ds(row, LAGS)] = lag_block(
            lefts, rights, None if base is None else base.at[j], a, c,
            high_table, low_table, cross_high, cross_low, unrolled,
        )

    over(blocks, LAGS, block, unrolled)
    return start - first * LAGS


def send_kernel(
    width, blocks, sends, x0, g1, xa, xb, dft, band, inverse, index, high_table, low_table,
    out, h1, cross_high, cross_low, lagged,
):
    x = jnp.concatenate([xa[...], xb[...]], axis=0)
    white = whiten_rows(x, dft[...], band[...], inverse[...], index[...])
    for c in range(3):
        h1[c] = white[c]
    for k in range(sends):
        base = x0.at[k * blocks : (k + 1) * blocks]
        shift = piece(
            lax.axis_index("tm") ^ (2 * (k + 1)), width, blocks, (g1,), (h1,), base, lagged,
            high_table, low_table, cross_high, cross_low, sends == 1,
        )
        out[k] = lagged[pl.ds(pl.multiple_of(shift, 16), width)].astype(BF16)


def own_kernel(
    width, blocks, g0, h0, g1, h1, high_table, low_table, out, cross_high, cross_low, lagged
):
    shift = piece(
        lax.axis_index("tm"), width, blocks, (g0, g1), (h0, h1), None, lagged,
        high_table, low_table, cross_high, cross_low, False,
    )
    out[...] = lagged[pl.ds(pl.multiple_of(shift, 16), width)]


def total_kernel(own, received, out):
    total = own[...]
    for j in range(received.shape[0]):
        total = total + received[j].astype(F32)
    out[...] = total.astype(BF16)


def ranks(owner, blocks):
    pairs = owner.shape[1]
    hits = lax.broadcasted_iota(jnp.int32, (blocks, pairs), 0) == owner
    hits = hits.astype(F32)
    earlier = lax.broadcasted_iota(jnp.int32, (pairs, pairs), 0) < lax.broadcasted_iota(jnp.int32, (pairs, pairs), 1)
    before = jnp.dot(hits.astype(BF16), earlier.astype(F32).astype(BF16), preferred_element_type=F32)
    return jnp.sum(before * hits, axis=0, keepdims=True).astype(jnp.int32)


def pick_kernel(blocks, capacity, owner, other_owner, out):
    me = lax.axis_index("sta")
    chip, core = me // 2, me % 2
    pairs = owner.shape[1]
    for place, (value, lists) in enumerate(((owner[...], core), (other_owner[...], 1 - core))):
        slot = ((value // 2) ^ chip) * (2 * capacity) + lists * capacity + ranks(value, blocks)
        mine = jnp.logical_and(value >= 0, value % 2 == core)
        slot = jnp.where(mine, slot, -1)
        slots = lax.broadcasted_iota(jnp.int32, (blocks * capacity, pairs), 0)
        out[:, place * pairs : (place + 1) * pairs] = (slots == slot).astype(F32).astype(BF16)


def route_kernel(total, other, pick, *outs):
    values = jnp.concatenate([total[...], other[...]], axis=1)
    routed = lax.dot_general(values, pick[...], (((1,), (1,)), ((), ())), preferred_element_type=F32)
    lanes = routed.shape[1] // len(outs)
    for j, out in enumerate(outs):
        out[...] = routed[:, j * lanes : (j + 1) * lanes].astype(BF16)


def place_kernel(lanes, top, *refs):
    out, rows, sems = refs[-3:]
    chip = lax.axis_index("sta") // 2
    copies = []
    for j in range(rows.shape[0]):
        at = pl.ds(pl.multiple_of((chip ^ j) * lanes, lanes), lanes)
        rows[j] = refs[j][...].astype(F32)
        copies.append(pltpu.make_async_copy(rows.at[j], out.at[pl.ds(top, rows.shape[1]), at], sems.at[j]))
        copies[-1].start()
    for copy in copies:
        copy.wait()


def place(lanes, top, shape, arrived, before):
    chips = len(arrived)
    args = list(arrived) + ([] if before is None else [before])
    anywhere = pl.BlockSpec(memory_space=pl.ANY)
    return pl.pallas_call(
        functools.partial(place_kernel, lanes, top),
        out_shape=shape,
        in_specs=[pl.BlockSpec(memory_space=pltpu.VMEM)] * chips + [anywhere] * (before is not None),
        out_specs=anywhere,
        scratch_shapes=[pltpu.VMEM((chips, arrived[0].shape[0], lanes), F32), pltpu.SemaphoreType.DMA((chips,))],
        input_output_aliases={} if before is None else {chips: 0},
        compiler_params=pltpu.CompilerParams(vmem_limit_bytes=VMEM_LIMIT),
        cost_estimate=pl.CostEstimate(flops=1024, bytes_accessed=1024, transcendentals=0),
    )(*args)


def call(kernel, out_shape, args, scratch=()):
    outs = jax.tree.map(lambda _: pl.BlockSpec(memory_space=pltpu.VMEM), out_shape)
    return pl.pallas_call(
        kernel,
        out_shape=out_shape,
        in_specs=[pl.BlockSpec(memory_space=pltpu.VMEM)] * len(args),
        out_specs=outs,
        scratch_shapes=list(scratch),
        compiler_params=pltpu.CompilerParams(vmem_limit_bytes=VMEM_LIMIT),
        cost_estimate=pl.CostEstimate(flops=1024, bytes_accessed=1024, transcendentals=0),
    )(*args)


def local(waves, partner, pair_count, left_station, right_station, owner):
    sta_count = lax.axis_size("sta")
    tm_count = lax.axis_size("tm")
    comps, stations, seg_local, samples = waves.shape
    freqs = samples // 2
    pairs = left_station.shape[1]
    capacity = 2 * pairs // sta_count
    width = comps * comps * LAGS // tm_count
    chips = sta_count // 2
    sends = tm_count // 2 - 1
    top = LAGS - math.gcd(width, LAGS)
    blocks = -(-(top + width) // LAGS)
    scale = 1.0 / math.sqrt(freqs * seg_local * tm_count)
    dft, high_table, low_table, band, inverse = (jnp.asarray(a) for a in tables(samples, freqs, scale))

    x = waves.reshape(comps * stations, samples)
    by_cross = -(-x.shape[0] * 5 // 8 // 16) * 16
    rows_shape = jax.ShapeDtypeStruct((comps, 2 * freqs, pairs), F32)

    def whitened(records, index):
        return call(
            whiten_kernel, rows_shape, (records, dft, band, inverse, index),
            [pltpu.VMEM((comps, 2 * freqs, stations), F32)],
        )

    def gather(offset, x, left, right, owner, pair_count):
        swap = functools.partial(lax.ppermute, axis_name="tm", perm=xor_pairs(tm_count, 1))
        cross = functools.partial(lax.ppermute, axis_name="sta", perm=xor_pairs(sta_count, offset))
        p = cross(x)
        x_next = swap(x)
        g0 = whitened(x, left)
        listed = jnp.where(jnp.arange(pairs, dtype=jnp.int32)[None, :] < pair_count[0], owner, -1)
        other_listed = lax.ppermute(listed, "sta", xor_pairs(sta_count, 1))
        pick = call(
            functools.partial(pick_kernel, sta_count, capacity),
            jax.ShapeDtypeStruct((sta_count * capacity, 2 * pairs), BF16),
            (listed, other_listed),
        )
        near, g0, pick = lax.optimization_barrier((x_next[:by_cross], g0, pick))
        pa = cross(near)
        pb = cross(x_next[by_cross:]) if offset == 1 else swap(p[by_cross:])
        g1 = whitened(x_next, left)
        p, g1 = lax.optimization_barrier((p, g1))
        h0 = whitened(p, right)
        x0 = call(
            functools.partial(cross_kernel, width, blocks, sends),
            jax.ShapeDtypeStruct((sends * blocks, 2 * freqs, pairs), F32),
            (g0, h0),
        )
        sent, h1 = call(
            functools.partial(send_kernel, width, blocks, sends),
            (
                jax.ShapeDtypeStruct((sends, width, pairs), BF16),
                rows_shape,
            ),
            (x0, g1, pa, pb, dft, band, inverse, right, high_table, low_table),
            scratch,
        )
        received = [lax.ppermute(sent[j], "tm", xor_pairs(tm_count, 2 * (j + 1))) for j in range(sends)]
        own = call(
            functools.partial(own_kernel, width, blocks),
            jax.ShapeDtypeStruct((width, pairs), F32),
            (g0, h0, g1, h1, high_table, low_table),
            scratch,
        )
        shape = jax.ShapeDtypeStruct((width, pairs), BF16)
        return call(total_kernel, shape, (own, jnp.stack(received))), pick

    scratch = [pltpu.VMEM((2 * freqs, pairs), BF16)] * 2 + [pltpu.VMEM((blocks * LAGS, pairs), F32)]
    branches = [functools.partial(gather, k) for k in range(1, sta_count)]
    summed, pick = lax.switch(
        partner.reshape(-1)[0] - 1, branches, x, left_station, right_station, owner, pair_count
    )
    lanes = 2 * capacity
    other = lax.ppermute(summed, "sta", xor_pairs(sta_count, 1))
    routed = call(route_kernel, [jax.ShapeDtypeStruct((width, lanes), BF16)] * chips, (summed, other, pick))
    arrived = [lax.ppermute(routed[j], "sta", xor_pairs(sta_count, 2 * j)) for j in range(chips - 1, 0, -1)]
    arrived = [routed[0]] + arrived[::-1]
    if lanes % 128 == 0:
        result = place(lanes, 0, jax.ShapeDtypeStruct((width, sta_count * capacity), F32), arrived, None)
    else:
        order = jnp.bitwise_xor(lax.axis_index("sta") // 2, jnp.arange(chips, dtype=jnp.int32))
        result = jnp.take(jnp.stack(arrived), order, axis=0).astype(F32)
        result = jnp.transpose(result, (1, 0, 2)).reshape(width, sta_count * capacity)
    return result.T


def solution(mesh):
    in_specs = (
        P(None, "sta", "tm", None),
        P(),
        P("sta"),
        P("sta", None),
        P("sta", None),
        P("sta", None),
    )
    out_specs = P("sta", "tm")
    return jax.shard_map(local, mesh=mesh, in_specs=in_specs, out_specs=out_specs, check_vma=False)
```
